256 devices in a mesh: leaf: 64 (over z, x, core), rhs: 4 (over y).
Axes of the slice: x: 4, y: 4, z: 8, core: 2. Of those that a mesh axis runs over, the one named last changes fastest.
Arguments:
- density: bfloat16 [16, 512, 384], P('rhs', 'leaf'), may hold values from -6 to 6
- near_blocks: bfloat16 [512, 16, 384, 384], P('leaf', 'rhs'), may hold values from -0.078125 to 0.078125
- near_send: int32 [64, 64, 1], P('leaf'), may hold values from 0 to 7, as said below
- near_slot: int32 [512, 16], P('leaf', 'rhs'), may hold values from 0 to 71, as said below
- col_basis: bfloat16 [512, 64, 384], P('leaf'), may hold values from -0.3125 to 0.3125
- up_transfer: bfloat16 [384, 64, 128], P('leaf'), may hold values from -0.5 to 0.5
- coupling: bfloat16 [896, 64, 1024], P('leaf', None, 'rhs'), may hold values from -0.1875 to 0.1875
- down_transfer: bfloat16 [384, 64, 128], P('leaf'), may hold values from -0.75 to 0.75
- row_basis: bfloat16 [512, 64, 384], P('leaf'), may hold values from -0.75 to 0.75
- coup_send: int32 [64, 64, 1], P('leaf'), may hold values from 0 to 13, as said below
- coup_slot: int32 [896, 16], P('leaf', 'rhs'), may hold values from 0 to 77, as said below
Outputs:
- velocity: bfloat16 [16, 512, 384], P('rhs', 'leaf')
The draws below stay inside these ranges and needn't reach their ends.
Inputs may be any that keep to these rules, and one draw needn't show every extreme that they name: `near_send`: entry [s, r, k] is a leaf of device s, numbered within s; for each s and r the 1 entries differ. `near_slot`: entry of device r's table: below 8 its own leaf of that number, else value - 8 = m names device m, and the entry stands for its leaf near_send[m, r, 0]. `coup_send`: entry [s, r, k] is a cluster of device s, numbered within s; for each s and r the 1 entries differ and have one level. `coup_slot`: entry of device r's table: below 14 its own cluster of that number, else value - 14 = m names device m, and the entry stands for its cluster coup_send[m, r, 0]; it has the same level as the row's cluster.
All inputs are finite; a program needn't handle non-finite values.
Results may differ from the reference program's by a relative error of at most 0.0056.
Values may be sent and summed in bfloat16 or wider, within the bound.
A program may use at most 64 MiB of HBM per device.

```python
import jax
import jax.numpy as jnp
from jax import lax

LEAF_DEV = 8
UNK = 384
RANK = 64
NRHS = 16
NNEAR = 16
NCOUP = 16
CAP = 1
CAPC = 1
CLUS_DEV = 14
PAR_DEV = 6
NLEAF = 512
CLUSTERS = 896
PARENTS = 384
N_LEAF = 64


def near_plan(key):
    base_key = jax.random.fold_in(key, 71)
    group_count = N_LEAF
    local_count = LEAF_DEV
    total_remote = group_count * CAP
    entries = local_count * NNEAR
    forced = min(total_remote, entries // 2)

    def per_group(receiver):
        group_key = jax.random.fold_in(base_key, receiver)
        shuffles = jax.vmap(lambda sender: jax.random.permutation(jax.random.fold_in(group_key, sender), local_count))(jnp.arange(group_count))
        outgoing = shuffles[:, :CAP].astype(jnp.int32)
        chosen = jax.random.randint(jax.random.fold_in(group_key, 5003), (entries,), 0, local_count + total_remote)
        ordinal = jax.random.permutation(jax.random.fold_in(group_key, 5005), total_remote)[:forced]
        places = jax.random.permutation(jax.random.fold_in(group_key, 5004), entries)[:forced]
        targets = chosen.at[places].set(local_count + ordinal)
        return (outgoing, targets.reshape(local_count, NNEAR).astype(jnp.int32))
    outgoing, targets = jax.vmap(per_group)(jnp.arange(group_count))
    return (jnp.transpose(outgoing, (1, 0, 2)).astype(jnp.int32), targets.reshape(group_count * local_count, NNEAR).astype(jnp.int32))


def level_of(distance):
    phase = distance % 4
    return jnp.where(phase < 2, 0, jnp.where(phase == 2, 1, 2))


def peer_distance(level_index, ordinal):
    if level_index == 0:
        return 4 * (ordinal // 2) + ordinal % 2
    if level_index == 1:
        return 4 * ordinal + 2
    return 4 * ordinal + 3


def far_plan(key):
    base_key = jax.random.fold_in(key, 83)
    group_count = N_LEAF
    sizes_level = (LEAF_DEV, LEAF_DEV // 2, LEAF_DEV // 4)
    peers_level = (group_count // 2, group_count // 4, group_count // 4)
    offsets_level = (0, LEAF_DEV, LEAF_DEV + LEAF_DEV // 2)

    def per_group(receiver):
        group_key = jax.random.fold_in(base_key, receiver)

        def listing(sender):
            sender_key = jax.random.fold_in(group_key, sender)
            level_here = level_of((sender - receiver) % group_count)
            pieces = []
            for level_index in range(3):
                shuffle = jax.random.permutation(jax.random.fold_in(sender_key, level_index), sizes_level[level_index])
                pieces.append(offsets_level[level_index] + shuffle[:CAPC])
            picked = jnp.where(level_here == 0, pieces[0], jnp.where(level_here == 1, pieces[1], pieces[2]))
            return picked.astype(jnp.int32)
        outgoing = jax.vmap(listing)(jnp.arange(group_count))
        levels_rows = []
        for level_index in range(3):
            local_count = sizes_level[level_index]
            eligible = peers_level[level_index] * CAPC
            entries = local_count * NCOUP
            forced = min(eligible, entries // 2)
            offset_cluster = offsets_level[level_index]

            def to_slot(drawn):
                remote = jnp.maximum(drawn - local_count, 0)
                ordinal = remote // CAPC
                within = remote % CAPC
                peer = (receiver + peer_distance(level_index, ordinal)) % group_count
                return jnp.where(drawn < local_count, offset_cluster + drawn, CLUS_DEV + peer * CAPC + within)
            chosen = jax.random.randint(jax.random.fold_in(group_key, 700 + level_index), (entries,), 0, local_count + eligible)
            picks = jax.random.permutation(jax.random.fold_in(group_key, 900 + level_index), eligible)[:forced]
            places = jax.random.permutation(jax.random.fold_in(group_key, 800 + level_index), entries)[:forced]
            chosen = chosen.at[places].set(local_count + picks)
            levels_rows.append(to_slot(chosen).reshape(local_count, NCOUP))
        return (outgoing, jnp.concatenate(levels_rows, axis=0).astype(jnp.int32))
    outgoing, targets = jax.vmap(per_group)(jnp.arange(group_count))
    return (jnp.transpose(outgoing, (1, 0, 2)).astype(jnp.int32), targets.reshape(group_count * CLUS_DEV, NCOUP).astype(jnp.int32))


def draw_near_send(key, part):
    outgoing, targets = near_plan(key)
    return outgoing


def draw_near_slot(key, part):
    outgoing, targets = near_plan(key)
    return targets


def draw_coup_send(key, part):
    outgoing, targets = far_plan(key)
    return outgoing


def draw_coup_slot(key, part):
    outgoing, targets = far_plan(key)
    return targets


def block_levels(rng, dims, shards, smallest, largest):
    def one(position, parts):
        steps = jax.random.uniform(jax.random.fold_in(jax.random.fold_in(rng, 6), position), (parts,), jnp.float32, smallest / len(shards), largest / len(shards))
        return jnp.repeat(jnp.exp(steps), dims[position] // parts).reshape((-1,) + (1,) * (len(dims) - position - 1))

    factor_of = one(*shards[0])
    for cut in shards[1:]:
        factor_of = factor_of * one(*cut)
    return factor_of


def gaussian(stream_key, extent, scale, limit, cuts=(), kind=jnp.bfloat16):
    values = jax.random.normal(stream_key, extent, jnp.float32) * scale
    if len(cuts) > 0:
        values = block_levels(stream_key, extent, cuts, -0.22, 0.18) * values
    return jnp.clip(values, min=-limit, max=limit).astype(kind)


def setup_inputs(seed: int = 0) -> dict:
    streams_of = jax.random.split(jax.random.key(seed), 12)
    return {
        "density": gaussian(streams_of[0], (NRHS, NLEAF, UNK), 1.0, 6.0, ((0, 4), (1, 64))),
        "near_blocks": gaussian(streams_of[1], (NLEAF, NNEAR, UNK, UNK), (UNK * NNEAR) ** -0.5, 0.078125, ((0, 64), (1, 4))),
        "near_send": draw_near_send(jax.random.fold_in(streams_of[11], 71), 0),
        "near_slot": draw_near_slot(jax.random.fold_in(streams_of[11], 71), 0),
        "col_basis": gaussian(streams_of[4], (NLEAF, RANK, UNK), UNK ** -0.5, 0.3125, ((0, 64),)),
        "up_transfer": gaussian(streams_of[5], (PARENTS, RANK, 2 * RANK), (2 * RANK) ** -0.5, 0.5, ((0, 64),)),
        "coupling": gaussian(streams_of[6], (CLUSTERS, RANK, NCOUP * RANK), (NCOUP * RANK) ** -0.5, 0.1875, ((0, 64), (2, 4))),
        "down_transfer": gaussian(streams_of[7], (PARENTS, RANK, 2 * RANK), RANK ** -0.5, 0.75, ((0, 64),)),
        "row_basis": gaussian(streams_of[8], (NLEAF, RANK, UNK), RANK ** -0.5, 0.75, ((0, 64),)),
        "coup_send": draw_coup_send(jax.random.fold_in(streams_of[11], 71), 0),
        "coup_slot": draw_coup_slot(jax.random.fold_in(streams_of[11], 71), 0),
    }


HIGHEST_PRECISION = lax.Precision.HIGHEST


def resolve(table_slots, listing, local_count, per_peer):
    owner = (jnp.arange(table_slots.shape[0], dtype=jnp.int32) // local_count)[:, None]
    owner = jnp.broadcast_to(owner, table_slots.shape).astype(jnp.int32)
    remote = jnp.maximum(table_slots - local_count, 0)
    sender = (remote // per_peer).astype(jnp.int32)
    within = (remote % per_peer).astype(jnp.int32)
    listed = listing[sender, owner, within]
    return jnp.where(table_slots < local_count, owner * local_count + table_slots, sender * local_count + listed).astype(jnp.int32)


def reference(density, near_blocks, near_send, near_slot, col_basis, up_transfer, coupling, down_transfer, row_basis, coup_send, coup_slot):
    group_count = N_LEAF
    half_count = LEAF_DEV // 2
    quarter = LEAF_DEV // 4
    by_leaf = jnp.transpose(density, (1, 0, 2))
    fine_charges = jnp.einsum('lru,lsu->lrs', col_basis.astype(jnp.float32), by_leaf.astype(jnp.float32)).astype(jnp.bfloat16)
    up_wide = up_transfer.astype(jnp.float32).reshape(group_count, PAR_DEV, RANK, 2 * RANK)
    pairs_fine = fine_charges.astype(jnp.float32).reshape(group_count, half_count, 2 * RANK, NRHS)
    mid_charges = jnp.einsum('gprc,gpcs->gprs', up_wide[:, :half_count], pairs_fine).astype(jnp.bfloat16)
    pairs_mid = mid_charges.astype(jnp.float32).reshape(group_count, quarter, 2 * RANK, NRHS)
    top_charges = jnp.einsum('gprc,gpcs->gprs', up_wide[:, half_count:], pairs_mid).astype(jnp.bfloat16)
    charges = jnp.concatenate([fine_charges.reshape(group_count, LEAF_DEV, RANK, NRHS), mid_charges, top_charges], axis=1)
    charges = charges.reshape(CLUSTERS, RANK, NRHS)
    sources = resolve(coup_slot, coup_send, CLUS_DEV, CAPC)
    gathered = charges[sources].reshape(CLUSTERS, NCOUP * RANK, NRHS)
    coupled = jnp.einsum('grc,gcs->grs', coupling.astype(jnp.float32), gathered.astype(jnp.float32))
    coupled = coupled.reshape(group_count, CLUS_DEV, RANK, NRHS)
    down_wide = down_transfer.astype(jnp.float32).reshape(group_count, PAR_DEV, RANK, 2 * RANK)
    coarse = coupled[:, LEAF_DEV + half_count:]
    middle = coupled[:, LEAF_DEV:LEAF_DEV + half_count] + jnp.einsum('gprc,gprs->gpcs', down_wide[:, half_count:], coarse, precision=HIGHEST_PRECISION).reshape(group_count, half_count, RANK, NRHS)
    finest = coupled[:, :LEAF_DEV] + jnp.einsum('gprc,gprs->gpcs', down_wide[:, :half_count], middle, precision=HIGHEST_PRECISION).reshape(group_count, LEAF_DEV, RANK, NRHS)
    far_part = jnp.einsum('lru,lrs->slu', row_basis.astype(jnp.float32), finest.reshape(NLEAF, RANK, NRHS), precision=HIGHEST_PRECISION)
    columns = resolve(near_slot, near_send, LEAF_DEV, CAP)

    def per_leaf(item):
        blocks, chosen = item
        picked = by_leaf[chosen].astype(jnp.float32)
        return jnp.einsum('kvu,ksu->sv', blocks.astype(jnp.float32), picked)

    near_part = lax.map(per_leaf, (near_blocks, columns))
    velocity = jnp.transpose(near_part, (1, 0, 2)) + far_part
    return velocity.astype(jnp.bfloat16)
```

```python
import functools

import jax
import jax.numpy as jnp
from jax import lax
from jax.experimental import pallas as pl
from jax.experimental.pallas import tpu as pltpu
from jax.sharding import PartitionSpec as P

BF = jnp.bfloat16
F32 = jnp.float32
MESH = pl.DeviceIdType.MESH
NT = (((1,), (1,)), ((), ()))
NN = (((1,), (0,)), ((), ()))
ORDER = (12, 13, 8, 9, 10, 11, 0, 1, 2, 3, 4, 5, 6, 7)
CHUNKS = 4
PER = 32 // CHUNKS


def dot(a, b, dims=NN):
    return lax.dot_general(a, b, dims, preferred_element_type=F32)


def iota(shape, axis):
    return lax.broadcasted_iota(jnp.int32, shape, axis)


def kernel(
    n_leaf,
    near_send,
    coup_send,
    near_slot,
    coup_slot,
    density_h,
    near_h,
    col_h,
    up_h,
    coupling_h,
    down_h,
    row_h,
    out,
    density,
    near,
    col,
    up,
    coupling,
    down,
    row,
    slots,
    slots_s,
    tiles,
    charges,
    table,
    send1,
    send2,
    recv2,
    send4,
    recv4,
    in_sem,
    near_sem,
    smem_sem,
    s0_send,
    s0_recv,
    s1_send,
    s1_recv,
    s2_send,
    s2_recv,
    s4_send,
    s4_recv,
):
    me = lax.axis_index("leaf")
    y = lax.axis_index("rhs")
    slow = ((density_h, density), (col_h, col), (up_h, up), (coupling_h, coupling), (down_h, down), (row_h, row))
    loads = [pltpu.make_async_copy(a, b, in_sem.at[i]) for i, (a, b) in enumerate(slow)]
    for load in loads:
        load.start()
    blocks = [pltpu.make_async_copy(near_h.at[i], near.at[i], near_sem.at[i]) for i in range(8)]
    for load in blocks:
        load.start()

    barrier = pltpu.get_barrier_semaphore()

    def greet(j, _):
        pl.semaphore_signal(
            barrier, inc=1, device_id={"leaf": lax.rem(me + j, n_leaf)}, device_id_type=MESH
        )
        return 0

    lax.fori_loop(1, n_leaf, greet, 0)
    for e in range(1, 4):
        pl.semaphore_signal(barrier, inc=1, device_id={"rhs": lax.rem(y + e, 4)}, device_id_type=MESH)

    slots[0, :, :] = jnp.zeros((8, 128), jnp.int32)
    slots[0, 0:4, 0:8] = near_slot[...]
    slots[0, 4:8, 0:14] = coup_slot[...]

    for load in loads[:3]:
        load.wait()
    flat = density[...].reshape(32, 384)
    stacked = jnp.concatenate([flat[:, 128 * c : 128 * c + 128] for c in range(3)], axis=0)
    r, q = iota((128, 96), 0), iota((128, 96), 1)
    pick = (r % 16 < 12) & (q == (r % 16) // 4 * 32 + r % 4 * 8 + r // 16)
    tile = dot(jnp.where(pick, 1.0, 0.0).astype(BF), stacked).astype(BF)
    r, q = iota((128, 32), 0), iota((128, 32), 1)
    pick = (r % 16 >= 12) & (q == r % 4 * 8 + r // 16)
    low = dot(jnp.where(pick, 1.0, 0.0).astype(BF), flat).astype(BF)
    left = iota((16, 128), 1) < 64

    def twice(a):
        return jnp.concatenate([a, a], axis=0)

    level = [dot(low[16 * i : 16 * i + 16], twice(col[i]), NT) for i in range(8)]
    values = [a.astype(BF) for a in level]
    for base, count in ((0, 4), (4, 2)):
        level = [
            dot(
                jnp.where(left, level[2 * j].astype(BF).astype(F32), level[2 * j + 1].astype(BF).astype(F32)).astype(BF),
                twice(up[base + j]),
                NT,
            )
            for j in range(count)
        ]
        values += [a.astype(BF) for a in level]
    for i in range(14):
        charges[i] = values[i]
        if i < 8:
            tiles[i] = tile[16 * i : 16 * i + 16]
            table[i] = tile[16 * i : 16 * i + 16] + values[i]
        else:
            table[i] = values[i]

    pl.semaphore_wait(barrier, n_leaf + 2)

    slot_copies = [
        pltpu.make_async_remote_copy(
            slots.at[0],
            slots.at[e],
            s0_send.at[e - 1],
            s0_recv.at[e - 1],
            device_id={"rhs": lax.rem(y + e, 4)},
            device_id_type=MESH,
        )
        for e in range(1, 4)
    ]
    for copy in slot_copies:
        copy.start()

    def listed(peer):
        return tiles[near_send[0, 0, peer]] + charges[coup_send[0, 0, peer]]

    def post(j, _):
        peer = lax.rem(me + j, n_leaf)
        send1[peer] = listed(peer)
        pltpu.make_async_remote_copy(
            send1.at[peer],
            table.at[14 + me],
            s1_send,
            s1_recv,
            device_id={"leaf": peer},
            device_id_type=MESH,
        ).start()
        return 0

    lax.fori_loop(1, n_leaf, post, 0)
    table[14 + me] = listed(me)

    for copy in slot_copies:
        copy.wait_recv()
    to_smem = pltpu.make_async_copy(slots, slots_s, smem_sem)
    to_smem.start()
    to_smem.wait()

    everything = pltpu.make_async_remote_copy(
        send1.at[pl.ds(0, n_leaf - 1)],
        table.at[pl.ds(14, n_leaf - 1)],
        s1_send,
        s1_recv,
        device_id={"leaf": lax.rem(me + 1, n_leaf)},
        device_id_type=MESH,
    )
    everything.wait_recv()

    rows, lanes = iota((16, 128), 0), iota((16, 128), 1)
    mask_n = jnp.where(rows < 12, 1.0, 0.0).astype(BF)
    mask_a = jnp.where((rows >= 12) & (lanes < 64), 1.0, 0.0).astype(BF)
    mask_b = jnp.where((rows >= 12) & (lanes >= 64), 1.0, 0.0).astype(BF)

    def read(e, i):
        slot = slots_s[e, i % 4, i // 4]
        value = table[slot + jnp.where(slot >= 8, 6, 0)] * mask_n
        if i < 28:
            g, k = ORDER[i // 2], i % 2 * 2
            value += table[slots_s[e, 4 + k, g]] * mask_a + table[slots_s[e, 5 + k, g]] * mask_b
        return value

    sends = []
    for chunk in range(CHUNKS):
        span = pl.ds(chunk * PER, PER)
        for e in (2, 1, 3):
            for i in range(chunk * PER, chunk * PER + PER):
                send2[e - 1, i] = read(4 - e, i)
            copy = pltpu.make_async_remote_copy(
                send2.at[e - 1, span],
                recv2.at[e, span],
                s2_send.at[e - 1, chunk],
                s2_recv.at[e - 1, chunk],
                device_id={"rhs": lax.rem(y + e, 4)},
                device_id_type=MESH,
            )
            copy.start()
            sends.append(copy)
        for i in range(chunk * PER, chunk * PER + PER):
            recv2[0, i] = read(0, i)

    for load in loads[3:]:
        load.wait()

    top = iota((8, 128), 0) < 4

    def regroup(i):
        parts = [recv2[e, i].astype(F32) for e in range(4)]
        groups = []
        for h in (0, 8):
            x = [p[h : h + 8] for p in parts]
            z = [pltpu.roll(p, 4, 0) for p in x]
            groups.append([jnp.where(top, x[0], z[1]), jnp.where(top, x[2], z[3])])
            groups.append([jnp.where(top, z[0], x[1]), jnp.where(top, z[2], x[3])])
        return [jnp.concatenate(g, axis=0).astype(BF) for g in groups]

    total = [None] * 8
    field = {}
    for chunk in range(CHUNKS):
        for copy in sends[3 * chunk : 3 * chunk + 3]:
            copy.wait_recv()
        pairs = {}
        for leaf in range(chunk * PER // 4, chunk * PER // 4 + PER // 4):
            blocks[leaf].wait()
            value = None
            for k in range(4):
                g = regroup(4 * leaf + k)
                pairs[4 * leaf + k] = g[3]
                part = dot(jnp.concatenate(g[:3], axis=1), near[leaf, k], NT)
                value = part if value is None else value + part
            total[leaf] = value
        for i in pairs:
            if i < 28 and i % 2 == 0:
                g = ORDER[i // 2]
                field[g] = dot(jnp.concatenate([pairs[i], pairs[i + 1]], axis=1), coupling[g], NT)

    def gain(parent, index):
        return dot(field[parent].astype(BF), down[index])

    for base, children, count, first in ((12, 8, 2, 4), (8, 0, 4, 0)):
        for j in range(count):
            both = gain(base + j, first + j)
            field[children + 2 * j] += both[:, :64]
            field[children + 2 * j + 1] += both[:, 64:]
    whole = jnp.concatenate(
        [(total[i] + dot(field[i].astype(BF), row[i])).astype(BF) for i in range(8)], axis=0
    )
    r, q = iota((128, 128), 0), iota((128, 128), 1)
    pick = q == r % 8 * 16 + r // 32 * 4 + r // 8 % 4
    sorted_rows = dot(jnp.where(pick, 1.0, 0.0).astype(BF), whole)
    last = []
    for e in range(1, 4):
        send4[e - 1] = sorted_rows[32 * e : 32 * e + 32].astype(BF)
        copy = pltpu.make_async_remote_copy(
            send4.at[e - 1],
            recv4.at[3 - e],
            s4_send.at[e - 1],
            s4_recv.at[3 - e],
            device_id={"rhs": lax.rem(y + 4 - e, 4)},
            device_id_type=MESH,
        )
        copy.start()
        last.append(copy)
    for copy in last:
        copy.wait()
    result = sorted_rows[:32]
    for e in range(3):
        result += recv4[e].astype(F32)
    out[...] = result.astype(BF).reshape(4, 8, 384)

    for copy in slot_copies:
        copy.wait_send()
    everything.wait_send()
    for copy in sends:
        copy.wait_send()


def shards(n_leaf, density, near_blocks, near_send, near_slot, col, up, coupling, down, row, coup_send, coup_slot):
    smem = pl.BlockSpec(memory_space=pltpu.SMEM)
    vmem = pl.BlockSpec(memory_space=pltpu.VMEM)
    hbm = pl.BlockSpec(memory_space=pl.ANY)
    big = [density, near_blocks, col, up, coupling, down, row]
    dma = pltpu.SemaphoreType.DMA
    return pl.pallas_call(
        functools.partial(kernel, n_leaf),
        out_shape=jax.ShapeDtypeStruct((4, 8, 384), BF),
        in_specs=[smem, smem, vmem, vmem] + [hbm] * len(big),
        out_specs=vmem,
        scratch_shapes=[pltpu.VMEM(a.shape, a.dtype) for a in big]
        + [
            pltpu.VMEM((4, 8, 128), jnp.int32),
            pltpu.SMEM((4, 8, 128), jnp.int32),
            pltpu.VMEM((8, 16, 128), BF),
            pltpu.VMEM((14, 16, 128), BF),
            pltpu.VMEM((14 + n_leaf, 16, 128), BF),
            pltpu.VMEM((n_leaf, 16, 128), BF),
            pltpu.VMEM((3, 32, 16, 128), BF),
            pltpu.VMEM((4, 32, 16, 128), BF),
            pltpu.VMEM((3, 32, 384), BF),
            pltpu.VMEM((3, 32, 384), BF),
            dma((6,)),
            dma((8,)),
            dma,
            dma((3,)),
            dma((3,)),
            dma,
            dma,
            dma((3, CHUNKS)),
            dma((3, CHUNKS)),
            dma((3,)),
            dma((3,)),
        ],
        compiler_params=pltpu.CompilerParams(
            collective_id=0, has_side_effects=True, vmem_limit_bytes=62 * 1024 * 1024
        ),
    )(
        jnp.transpose(near_send, (0, 2, 1)),
        jnp.transpose(coup_send, (0, 2, 1)),
        near_slot.T,
        coup_slot.T,
        *big,
    )


def solution(mesh):
    placed = (
        P("rhs", "leaf", None),
        P("leaf", "rhs", None, None),
        P("leaf", None, None),
        P("leaf", "rhs"),
        P("leaf", None, None),
        P("leaf", None, None),
        P("leaf", None, "rhs"),
        P("leaf", None, None),
        P("leaf", None, None),
        P("leaf", None, None),
        P("leaf", "rhs"),
    )
    return jax.shard_map(
        functools.partial(shards, mesh.shape["leaf"]),
        mesh=mesh,
        in_specs=placed,
        out_specs=P("rhs", "leaf", None),
        check_vma=False,
    )
```

```python
import functools

import jax
import jax.numpy as jnp
from jax import lax
from jax.experimental import pallas as pl
from jax.experimental.pallas import tpu as pltpu
from jax.sharding import PartitionSpec as P

BF = jnp.bfloat16
F32 = jnp.float32
MESH = pl.DeviceIdType.MESH
NT = (((1,), (1,)), ((), ()))
NN = (((1,), (0,)), ((), ()))
ORDER = (12, 13, 8, 9, 10, 11, 0, 1, 2, 3, 4, 5, 6, 7)
CHUNKS = (2, 4)


def dot(a, b, dims=NN):
    return lax.dot_general(a, b, dims, preferred_element_type=F32)


def iota(shape, axis):
    return lax.broadcasted_iota(jnp.int32, shape, axis)


def kernel(
    n_leaf,
    near_send_h,
    coup_send_h,
    near_slot_h,
    coup_slot_h,
    density_h,
    near_h,
    col_h,
    up_h,
    coupling_h,
    down_h,
    row_h,
    out,
    near_send,
    coup_send,
    near_slot,
    coup_slot,
    density,
    near,
    col,
    up,
    coupling,
    down,
    row,
    slots,
    slots_s,
    tiles,
    charges,
    table_a,
    table_b,
    send1,
    send2,
    recv2,
    send4,
    recv4,
    in_sem,
    near_sem,
    smem_sem,
    s0_send,
    s0_recv,
    s1_send,
    s1_recv,
    s2_send,
    s2_recv,
    s4_send,
    s4_recv,
):
    me = lax.axis_index("leaf")
    y = lax.axis_index("rhs")
    first = (
        (density_h, density),
        (col_h, col),
        (near_send_h, near_send),
        (coup_send_h, coup_send),
        (near_slot_h, near_slot),
        (coup_slot_h, coup_slot),
        (up_h, up),
    )
    later = ((coupling_h, coupling), (down_h, down), (row_h, row))
    loads = [pltpu.make_async_copy(a, b, in_sem.at[i]) for i, (a, b) in enumerate(first + later)]
    for load in loads[:7]:
        load.start()

    barrier = pltpu.get_barrier_semaphore()
    zs = [lax.rem(me // 8 + dz, n_leaf // 8) * 8 for dz in range(n_leaf // 8)]
    xs = [lax.rem(me // 2 % 4 + w // 2, 4) * 2 + lax.rem(me % 2 + w % 2, 2) for w in range(8)]
    far_z = sorted(range(n_leaf // 8), key=lambda dz: -min(dz, n_leaf // 8 - dz))
    far_x = (5, 4, 3, 2, 7, 6, 1, 0)
    for dz, w in [(dz, w) for dz in far_z for w in far_x if dz or w]:
        pl.semaphore_signal(barrier, inc=1, device_id={"leaf": zs[dz] + xs[w]}, device_id_type=MESH)
    for e in range(1, 4):
        pl.semaphore_signal(barrier, inc=1, device_id={"rhs": lax.rem(y + e, 4)}, device_id_type=MESH)

    blocks = [pltpu.make_async_copy(near_h.at[i], near.at[i], near_sem.at[i]) for i in range(8)]
    for load in loads[7:] + blocks:
        load.start()

    for load in loads[:7]:
        load.wait()
    slots[0, :, :] = jnp.zeros((8, 128), jnp.int32)
    slots[0, 0:4, 0:8] = near_slot[...]
    slots[0, 4:8, 0:14] = coup_slot[...]

    flat = density[...].reshape(32, 384)
    stacked = jnp.concatenate([flat[:, 128 * c : 128 * c + 128] for c in range(3)], axis=0)
    r, q = iota((128, 96), 0), iota((128, 96), 1)
    source = r % 4 * 8 + r % 64 // 8
    pick = (r < 64) & (q == source + r // 4 % 2 * 32) | (r >= 64) & (r % 8 < 4) & (q == source + 64)
    tile = dot(jnp.where(pick, 1.0, 0.0).astype(BF), stacked)
    r, q = iota((128, 32), 0), iota((128, 32), 1)
    pick = (r % 16 >= 4) & (r % 16 < 8) & (q == r % 4 * 8 + r // 16)
    low = dot(jnp.where(pick, 1.0, 0.0).astype(BF), flat).astype(BF)
    left = iota((16, 128), 1) < 64

    def twice(a):
        return jnp.concatenate([a, a], axis=0)

    level = [dot(low[16 * i : 16 * i + 16], twice(col[i]), NT) for i in range(8)]
    level_values = [a.astype(BF).astype(F32) for a in level]
    for base, count in ((0, 4), (4, 2)):
        level = [
            dot(
                jnp.where(left, level[2 * j].astype(BF).astype(F32), level[2 * j + 1].astype(BF).astype(F32)).astype(BF),
                twice(up[base + j]),
                NT,
            )
            for j in range(count)
        ]
        level_values += [a.astype(BF).astype(F32) for a in level]
    for i in range(14):
        value = level_values[i][:8]
        charges[i] = value.astype(BF)
        if i < 8:
            tiles[0, i] = tile[8 * i : 8 * i + 8].astype(BF)
            tiles[1, i] = tile[64 + 8 * i : 72 + 8 * i].astype(BF)
            table_a[i] = tile[8 * i : 8 * i + 8].astype(BF)
            value += tile[64 + 8 * i : 72 + 8 * i]
        table_b[i] = value.astype(BF)

    def listed(peer, _):
        leaf = near_send[0, 0, peer]
        send1[0, peer] = tiles[0, leaf]
        send1[1, peer] = tiles[1, leaf] + charges[coup_send[0, 0, peer]]
        return 0

    lax.fori_loop(0, n_leaf, listed, 0, unroll=8)
    pl.semaphore_wait(barrier, n_leaf + 2)

    slot_copies = [
        pltpu.make_async_remote_copy(
            slots.at[0],
            slots.at[e],
            s0_send.at[e - 1],
            s0_recv.at[e - 1],
            device_id={"rhs": lax.rem(y + e, 4)},
            device_id_type=MESH,
        )
        for e in range(1, 4)
    ]
    for copy in slot_copies:
        copy.start()

    tables = ((table_a, 8), (table_b, 14))
    for half, (table, own) in enumerate(tables):
        for dz, w in [(dz, w) for w in far_x for dz in far_z if dz or w]:
            peer = zs[dz] + xs[w]
            pltpu.make_async_remote_copy(
                send1.at[half, peer],
                table.at[own + me],
                s1_send.at[half],
                s1_recv.at[half],
                device_id={"leaf": peer},
                device_id_type=MESH,
            ).start()
        table[own + me] = send1[half, me]

    for copy in slot_copies:
        copy.wait_recv()
    to_smem = pltpu.make_async_copy(slots, slots_s, smem_sem)
    to_smem.start()
    to_smem.wait()

    everything = [
        pltpu.make_async_remote_copy(
            send1.at[half, pl.ds(0, n_leaf - 1)],
            table.at[pl.ds(own, n_leaf - 1)],
            s1_send.at[half],
            s1_recv.at[half],
            device_id={"leaf": lax.rem(me + 1, n_leaf)},
            device_id_type=MESH,
        )
        for half, (table, own) in enumerate(tables)
    ]

    rows, lanes = iota((8, 128), 0), iota((8, 128), 1)
    mask_n = jnp.where(rows < 4, 1.0, 0.0).astype(BF)
    mask_a = jnp.where((rows >= 4) & (lanes < 64), 1.0, 0.0).astype(BF)
    mask_b = jnp.where((rows >= 4) & (lanes >= 64), 1.0, 0.0).astype(BF)

    def read(half, e, i):
        slot = slots_s[e, i % 4, i // 4]
        if half == 0:
            return table_a[slot]
        value = table_b[slot + jnp.where(slot >= 8, 6, 0)] * mask_n
        if i < 28:
            g, k = ORDER[i // 2], i % 2 * 2
            value += table_b[slots_s[e, 4 + k, g]] * mask_a + table_b[slots_s[e, 5 + k, g]] * mask_b
        return value

    sends = [[], []]
    for half in range(2):
        everything[half].wait_recv()
        per = 32 // CHUNKS[half]
        for chunk in range(CHUNKS[half]):
            span = pl.ds(chunk * per, per)
            for e in (2, 1, 3):
                for i in range(chunk * per, chunk * per + per):
                    send2[half, e - 1, i] = read(half, 4 - e, i)
                copy = pltpu.make_async_remote_copy(
                    send2.at[half, e - 1, span],
                    recv2.at[half, e, span],
                    s2_send.at[half, e - 1, chunk],
                    s2_recv.at[half, e - 1, chunk],
                    device_id={"rhs": lax.rem(y + e, 4)},
                    device_id_type=MESH,
                )
                copy.start()
                sends[half].append(copy)
        for i in range(32):
            recv2[half, 0, i] = read(half, 0, i)

    for load in loads[7:]:
        load.wait()

    top = iota((8, 128), 0) < 4

    def regroup(half, i):
        x = [recv2[half, e, i].astype(F32) for e in range(4)]
        z = [pltpu.roll(p, 4, 0) for p in x]
        groups = (
            [jnp.where(top, x[0], z[1]), jnp.where(top, x[2], z[3])],
            [jnp.where(top, z[0], x[1]), jnp.where(top, z[2], x[3])],
        )
        return [jnp.concatenate(g, axis=0).astype(BF) for g in groups]

    total = []
    for chunk in range(CHUNKS[0]):
        for copy in sends[0][3 * chunk : 3 * chunk + 3]:
            copy.wait_recv()
        for leaf in range(chunk * 8 // CHUNKS[0], (chunk + 1) * 8 // CHUNKS[0]):
            blocks[leaf].wait()
            value = None
            for k in range(4):
                part = dot(jnp.concatenate(regroup(0, 4 * leaf + k), axis=1), near[leaf, k, :, 0:256], NT)
                value = part if value is None else value + part
            total.append(value)

    field = {}
    for chunk in range(CHUNKS[1]):
        for copy in sends[1][3 * chunk : 3 * chunk + 3]:
            copy.wait_recv()
        pairs = {}
        for leaf in range(chunk * 8 // CHUNKS[1], (chunk + 1) * 8 // CHUNKS[1]):
            for k in (0, 2):
                one, two = regroup(1, 4 * leaf + k), regroup(1, 4 * leaf + k + 1)
                pairs[4 * leaf + k], pairs[4 * leaf + k + 1] = one[1], two[1]
                total[leaf] += dot(
                    jnp.concatenate([one[0], two[0]], axis=1),
                    jnp.concatenate([near[leaf, k, :, 256:384], near[leaf, k + 1, :, 256:384]], axis=1),
                    NT,
                )
        for i in pairs:
            if i < 28 and i % 2 == 0:
                g = ORDER[i // 2]
                field[g] = dot(jnp.concatenate([pairs[i], pairs[i + 1]], axis=1), coupling[g], NT)

    def gain(parent, index):
        return dot(field[parent].astype(BF), down[index])

    for base, children, count, first in ((12, 8, 2, 4), (8, 0, 4, 0)):
        for j in range(count):
            both = gain(base + j, first + j)
            field[children + 2 * j] += both[:, :64]
            field[children + 2 * j + 1] += both[:, 64:]
    whole = jnp.concatenate(
        [(total[i] + dot(field[i].astype(BF), row[i])).astype(BF) for i in range(8)], axis=0
    )
    r, q = iota((128, 128), 0), iota((128, 128), 1)
    pick = q == r % 8 * 16 + r // 32 * 4 + r // 8 % 4
    sorted_rows = dot(jnp.where(pick, 1.0, 0.0).astype(BF), whole)
    last = []
    for e in range(1, 4):
        send4[e - 1] = sorted_rows[32 * e : 32 * e + 32].astype(BF)
        copy = pltpu.make_async_remote_copy(
            send4.at[e - 1],
            recv4.at[3 - e],
            s4_send.at[e - 1],
            s4_recv.at[3 - e],
            device_id={"rhs": lax.rem(y + 4 - e, 4)},
            device_id_type=MESH,
        )
        copy.start()
        last.append(copy)
    for copy in last:
        copy.wait()
    result = sorted_rows[:32]
    for e in range(3):
        result += recv4[e].astype(F32)
    out[...] = result.astype(BF).reshape(4, 8, 384)

    for copy in slot_copies:
        copy.wait_send()
    for copy in everything + sends[0] + sends[1]:
        copy.wait_send()


def shards(n_leaf, density, near_blocks, near_send, near_slot, col, up, coupling, down, row, coup_send, coup_slot):
    vmem = pl.BlockSpec(memory_space=pltpu.VMEM)
    hbm = pl.BlockSpec(memory_space=pl.ANY)
    big = [density, near_blocks, col, up, coupling, down, row]
    dma = pltpu.SemaphoreType.DMA
    return pl.pallas_call(
        functools.partial(kernel, n_leaf),
        out_shape=jax.ShapeDtypeStruct((4, 8, 384), BF),
        in_specs=[hbm] * (4 + len(big)),
        out_specs=vmem,
        scratch_shapes=[
            pltpu.SMEM((1, 1, n_leaf), jnp.int32),
            pltpu.SMEM((1, 1, n_leaf), jnp.int32),
            pltpu.VMEM((4, 8), jnp.int32),
            pltpu.VMEM((4, 14), jnp.int32),
        ]
        + [pltpu.VMEM(a.shape, a.dtype) for a in big]
        + [
            pltpu.VMEM((4, 8, 128), jnp.int32),
            pltpu.SMEM((4, 8, 128), jnp.int32),
            pltpu.VMEM((2, 8, 8, 128), BF),
            pltpu.VMEM((14, 8, 128), BF),
            pltpu.VMEM((8 + n_leaf, 8, 128), BF),
            pltpu.VMEM((14 + n_leaf, 8, 128), BF),
            pltpu.VMEM((2, n_leaf, 8, 128), BF),
            pltpu.VMEM((2, 3, 32, 8, 128), BF),
            pltpu.VMEM((2, 4, 32, 8, 128), BF),
            pltpu.VMEM((3, 32, 384), BF),
            pltpu.VMEM((3, 32, 384), BF),
            dma((10,)),
            dma((8,)),
            dma,
            dma((3,)),
            dma((3,)),
            dma((2,)),
            dma((2,)),
            dma((2, 3, max(CHUNKS))),
            dma((2, 3, max(CHUNKS))),
            dma((3,)),
            dma((3,)),
        ],
        compiler_params=pltpu.CompilerParams(
            collective_id=0, has_side_effects=True, vmem_limit_bytes=62 * 1024 * 1024
        ),
    )(
        jnp.transpose(near_send, (0, 2, 1)),
        jnp.transpose(coup_send, (0, 2, 1)),
        near_slot.T,
        coup_slot.T,
        *big,
    )


def solution(mesh):
    placed = (
        P("rhs", "leaf", None),
        P("leaf", "rhs", None, None),
        P("leaf", None, None),
        P("leaf", "rhs"),
        P("leaf", None, None),
        P("leaf", None, None),
        P("leaf", None, "rhs"),
        P("leaf", None, None),
        P("leaf", None, None),
        P("leaf", None, None),
        P("leaf", "rhs"),
    )
    return jax.shard_map(
        functools.partial(shards, mesh.shape["leaf"]),
        mesh=mesh,
        in_specs=placed,
        out_specs=P("rhs", "leaf", None),
        check_vma=False,
    )
```

```python
import functools

import jax
import jax.numpy as jnp
from jax import lax
from jax.experimental import pallas as pl
from jax.experimental.pallas import tpu as pltpu
from jax.sharding import PartitionSpec as P

BF = jnp.bfloat16
F32 = jnp.float32
MESH = pl.DeviceIdType.MESH
NT = (((1,), (1,)), ((), ()))
NN = (((1,), (0,)), ((), ()))
ORDER = (12, 13, 8, 9, 10, 11, 0, 1, 2, 3, 4, 5, 6, 7)
CHUNKS = (2, 2)


def dot(a, b, dims=NN):
    return lax.dot_general(a, b, dims, preferred_element_type=F32)


def iota(shape, axis):
    return lax.broadcasted_iota(jnp.int32, shape, axis)


def kernel(
    n_leaf,
    near_send_h,
    coup_send_h,
    near_slot_h,
    coup_slot_h,
    density_h,
    near_h,
    col_h,
    up_h,
    coupling_h,
    down_h,
    row_h,
    out,
    near_send,
    coup_send,
    near_slot,
    coup_slot,
    density,
    near,
    col,
    up,
    coupling,
    down,
    row,
    slots,
    slots_s,
    tiles,
    charges,
    table_a,
    table_b,
    send1,
    send2,
    recv2,
    send4,
    recv4,
    in_sem,
    near_sem,
    smem_sem,
    s0_send,
    s0_recv,
    s1_send,
    s1_recv,
    s2_send,
    s2_recv,
    s4_send,
    s4_recv,
):
    me = lax.axis_index("leaf")
    y = lax.axis_index("rhs")
    first = (
        (density_h, density),
        (col_h, col),
        (near_send_h, near_send),
        (coup_send_h, coup_send),
        (near_slot_h, near_slot),
        (coup_slot_h, coup_slot),
        (up_h, up),
    )
    later = ((coupling_h, coupling), (down_h, down), (row_h, row))
    loads = [pltpu.make_async_copy(a, b, in_sem.at[i]) for i, (a, b) in enumerate(first + later)]
    for load in loads[:7]:
        load.start()

    barrier = pltpu.get_barrier_semaphore()
    zs = [lax.rem(me // 8 + dz, n_leaf // 8) * 8 for dz in range(n_leaf // 8)]
    xs = [lax.rem(me // 2 % 4 + w // 2, 4) * 2 + lax.rem(me % 2 + w % 2, 2) for w in range(8)]
    far_z = sorted(range(n_leaf // 8), key=lambda dz: -min(dz, n_leaf // 8 - dz))
    far_x = (5, 4, 3, 2, 7, 6, 1, 0)
    for dz, w in [(dz, w) for dz in far_z for w in far_x if dz or w]:
        pl.semaphore_signal(barrier, inc=1, device_id={"leaf": zs[dz] + xs[w]}, device_id_type=MESH)
    for e in range(1, 4):
        pl.semaphore_signal(barrier, inc=1, device_id={"rhs": lax.rem(y + e, 4)}, device_id_type=MESH)

    blocks = [pltpu.make_async_copy(near_h.at[i], near.at[i], near_sem.at[i]) for i in range(8)]
    for load in loads[7:] + blocks:
        load.start()

    for load in loads[:7]:
        load.wait()
    slots[0, :, :] = jnp.zeros((8, 128), jnp.int32)
    slots[0, 0:4, 0:8] = near_slot[...]
    slots[0, 4:8, 0:14] = coup_slot[...]

    flat = density[...].reshape(32, 384)
    stacked = jnp.concatenate([flat[:, 128 * c : 128 * c + 128] for c in range(3)], axis=0)
    r, q = iota((128, 96), 0), iota((128, 96), 1)
    source = r % 4 * 8 + r % 64 // 8
    pick = (r < 64) & (r % 8 < 4) & (q == source) | (r >= 64) & (q == source + 32 + r // 4 % 2 * 32)
    tile = dot(jnp.where(pick, 1.0, 0.0).astype(BF), stacked)
    r, q = iota((128, 32), 0), iota((128, 32), 1)
    pick = (r % 16 >= 4) & (r % 16 < 8) & (q == r % 4 * 8 + r // 16)
    low = dot(jnp.where(pick, 1.0, 0.0).astype(BF), flat).astype(BF)
    left = iota((16, 128), 1) < 64

    def twice(a):
        return jnp.concatenate([a, a], axis=0)

    level = [dot(low[16 * i : 16 * i + 16], twice(col[i]), NT) for i in range(8)]
    level_values = [a.astype(BF).astype(F32) for a in level]
    for base, count in ((0, 4), (4, 2)):
        level = [
            dot(
                jnp.where(left, level[2 * j].astype(BF).astype(F32), level[2 * j + 1].astype(BF).astype(F32)).astype(BF),
                twice(up[base + j]),
                NT,
            )
            for j in range(count)
        ]
        level_values += [a.astype(BF).astype(F32) for a in level]
    for i in range(14):
        value = level_values[i][:8]
        charges[i] = value.astype(BF)
        if i < 8:
            tiles[0, i] = tile[8 * i : 8 * i + 8].astype(BF)
            tiles[1, i] = tile[64 + 8 * i : 72 + 8 * i].astype(BF)
            table_b[i] = tile[64 + 8 * i : 72 + 8 * i].astype(BF)
            value += tile[8 * i : 8 * i + 8]
        table_a[i] = value.astype(BF)

    def listed(peer, _):
        leaf = near_send[0, 0, peer]
        send1[0, peer] = tiles[0, leaf] + charges[coup_send[0, 0, peer]]
        send1[1, peer] = tiles[1, leaf]
        return 0

    lax.fori_loop(0, n_leaf, listed, 0, unroll=8)
    pl.semaphore_wait(barrier, n_leaf + 2)

    slot_copies = [
        pltpu.make_async_remote_copy(
            slots.at[0],
            slots.at[e],
            s0_send.at[e - 1],
            s0_recv.at[e - 1],
            device_id={"rhs": lax.rem(y + e, 4)},
            device_id_type=MESH,
        )
        for e in range(1, 4)
    ]
    for copy in slot_copies:
        copy.start()

    tables = ((table_a, 14), (table_b, 8))
    for half, (table, own) in enumerate(tables):
        for dz, w in [(dz, w) for w in far_x for dz in far_z if dz or w]:
            peer = zs[dz] + xs[w]
            pltpu.make_async_remote_copy(
                send1.at[half, peer],
                table.at[own + me],
                s1_send.at[half],
                s1_recv.at[half],
                device_id={"leaf": peer},
                device_id_type=MESH,
            ).start()
        table[own + me] = send1[half, me]

    for copy in slot_copies:
        copy.wait_recv()
    to_smem = pltpu.make_async_copy(slots, slots_s, smem_sem)
    to_smem.start()
    to_smem.wait()

    everything = [
        pltpu.make_async_remote_copy(
            send1.at[half, pl.ds(0, n_leaf - 1)],
            table.at[pl.ds(own, n_leaf - 1)],
            s1_send.at[half],
            s1_recv.at[half],
            device_id={"leaf": lax.rem(me + 1, n_leaf)},
            device_id_type=MESH,
        )
        for half, (table, own) in enumerate(tables)
    ]

    rows, lanes = iota((8, 128), 0), iota((8, 128), 1)
    mask_n = jnp.where(rows < 4, 1.0, 0.0).astype(BF)
    mask_a = jnp.where((rows >= 4) & (lanes < 64), 1.0, 0.0).astype(BF)
    mask_b = jnp.where((rows >= 4) & (lanes >= 64), 1.0, 0.0).astype(BF)

    def read(half, e, i):
        slot = slots_s[e, i % 4, i // 4]
        if half == 1:
            return table_b[slot]
        value = table_a[slot + jnp.where(slot >= 8, 6, 0)] * mask_n
        if i < 28:
            g, k = ORDER[i // 2], i % 2 * 2
            value += table_a[slots_s[e, 4 + k, g]] * mask_a + table_a[slots_s[e, 5 + k, g]] * mask_b
        return value

    sends = [[], []]
    for half in range(2):
        everything[half].wait_recv()
        per = 32 // CHUNKS[half]
        for chunk in range(CHUNKS[half]):
            span = pl.ds(chunk * per, per)
            for e in (1, 3, 2):
                for i in range(chunk * per, chunk * per + per):
                    send2[half, e - 1, i] = read(half, 4 - e, i)
                copy = pltpu.make_async_remote_copy(
                    send2.at[half, e - 1, span],
                    recv2.at[half, e, span],
                    s2_send.at[half, e - 1, chunk],
                    s2_recv.at[half, e - 1, chunk],
                    device_id={"rhs": lax.rem(y + e, 4)},
                    device_id_type=MESH,
                )
                copy.start()
                sends[half].append(copy)
        for i in range(32):
            recv2[half, 0, i] = read(half, 0, i)

    for load in loads[7:]:
        load.wait()

    top = iota((8, 128), 0) < 4

    def regroup(half, i):
        x = [recv2[half, e, i].astype(F32) for e in range(4)]
        z = [pltpu.roll(p, 4, 0) for p in x]
        groups = (
            [jnp.where(top, x[0], z[1]), jnp.where(top, x[2], z[3])],
            [jnp.where(top, z[0], x[1]), jnp.where(top, z[2], x[3])],
        )
        return [jnp.concatenate(g, axis=0).astype(BF) for g in groups]

    def arrived(half, chunk):
        for copy in sends[half][3 * chunk : 3 * chunk + 3]:
            copy.wait_recv()
        return range(chunk * 8 // CHUNKS[half], (chunk + 1) * 8 // CHUNKS[half])

    pairs, total = {}, []
    for chunk in range(CHUNKS[0]):
        for leaf in arrived(0, chunk):
            blocks[leaf].wait()
            value = None
            for k in (0, 2):
                one, two = regroup(0, 4 * leaf + k), regroup(0, 4 * leaf + k + 1)
                pairs[4 * leaf + k], pairs[4 * leaf + k + 1] = one[1], two[1]
                part = dot(
                    jnp.concatenate([one[0], two[0]], axis=1),
                    jnp.concatenate([near[leaf, k, :, 0:128], near[leaf, k + 1, :, 0:128]], axis=1),
                    NT,
                )
                value = part if value is None else value + part
            total.append(value)

    field = {}
    for j, g in enumerate(ORDER):
        field[g] = dot(jnp.concatenate([pairs[2 * j], pairs[2 * j + 1]], axis=1), coupling[g], NT)
    for base, children, count, first in ((12, 8, 2, 4), (8, 0, 4, 0)):
        for j in range(count):
            both = dot(field[base + j].astype(BF), down[first + j])
            field[children + 2 * j] += both[:, :64]
            field[children + 2 * j + 1] += both[:, 64:]
    for i in range(8):
        total[i] += dot(field[i].astype(BF), row[i])

    for chunk in range(CHUNKS[1]):
        for leaf in arrived(1, chunk):
            for k in range(4):
                total[leaf] += dot(
                    jnp.concatenate(regroup(1, 4 * leaf + k), axis=1), near[leaf, k, :, 128:384], NT
                )
    whole = jnp.concatenate([value.astype(BF) for value in total], axis=0)
    r, q = iota((128, 128), 0), iota((128, 128), 1)
    pick = q == r % 8 * 16 + r // 32 * 4 + r // 8 % 4
    sorted_rows = dot(jnp.where(pick, 1.0, 0.0).astype(BF), whole)
    last = []
    for e in range(1, 4):
        send4[e - 1] = sorted_rows[32 * e : 32 * e + 32].astype(BF)
        copy = pltpu.make_async_remote_copy(
            send4.at[e - 1],
            recv4.at[3 - e],
            s4_send.at[e - 1],
            s4_recv.at[3 - e],
            device_id={"rhs": lax.rem(y + 4 - e, 4)},
            device_id_type=MESH,
        )
        copy.start()
        last.append(copy)
    for copy in last:
        copy.wait()
    result = sorted_rows[:32]
    for e in range(3):
        result += recv4[e].astype(F32)
    out[...] = result.astype(BF).reshape(4, 8, 384)

    for copy in slot_copies:
        copy.wait_send()
    for copy in everything + sends[0] + sends[1]:
        copy.wait_send()


def shards(n_leaf, density, near_blocks, near_send, near_slot, col, up, coupling, down, row, coup_send, coup_slot):
    vmem = pl.BlockSpec(memory_space=pltpu.VMEM)
    hbm = pl.BlockSpec(memory_space=pl.ANY)
    big = [density, near_blocks, col, up, coupling, down, row]
    dma = pltpu.SemaphoreType.DMA
    return pl.pallas_call(
        functools.partial(kernel, n_leaf),
        out_shape=jax.ShapeDtypeStruct((4, 8, 384), BF),
        in_specs=[hbm] * (4 + len(big)),
        out_specs=vmem,
        scratch_shapes=[
            pltpu.SMEM((1, 1, n_leaf), jnp.int32),
            pltpu.SMEM((1, 1, n_leaf), jnp.int32),
            pltpu.VMEM((4, 8), jnp.int32),
            pltpu.VMEM((4, 14), jnp.int32),
        ]
        + [pltpu.VMEM(a.shape, a.dtype) for a in big]
        + [
            pltpu.VMEM((4, 8, 128), jnp.int32),
            pltpu.SMEM((4, 8, 128), jnp.int32),
            pltpu.VMEM((2, 8, 8, 128), BF),
            pltpu.VMEM((14, 8, 128), BF),
            pltpu.VMEM((14 + n_leaf, 8, 128), BF),
            pltpu.VMEM((8 + n_leaf, 8, 128), BF),
            pltpu.VMEM((2, n_leaf, 8, 128), BF),
            pltpu.VMEM((2, 3, 32, 8, 128), BF),
            pltpu.VMEM((2, 4, 32, 8, 128), BF),
            pltpu.VMEM((3, 32, 384), BF),
            pltpu.VMEM((3, 32, 384), BF),
            dma((10,)),
            dma((8,)),
            dma,
            dma((3,)),
            dma((3,)),
            dma((2,)),
            dma((2,)),
            dma((2, 3, max(CHUNKS))),
            dma((2, 3, max(CHUNKS))),
            dma((3,)),
            dma((3,)),
        ],
        compiler_params=pltpu.CompilerParams(
            collective_id=0, has_side_effects=True, vmem_limit_bytes=62 * 1024 * 1024
        ),
    )(
        jnp.transpose(near_send, (0, 2, 1)),
        jnp.transpose(coup_send, (0, 2, 1)),
        near_slot.T,
        coup_slot.T,
        *big,
    )


def solution(mesh):
    placed = (
        P("rhs", "leaf", None),
        P("leaf", "rhs", None, None),
        P("leaf", None, None),
        P("leaf", "rhs"),
        P("leaf", None, None),
        P("leaf", None, None),
        P("leaf", None, "rhs"),
        P("leaf", None, None),
        P("leaf", None, None),
        P("leaf", None, None),
        P("leaf", "rhs"),
    )
    return jax.shard_map(
        functools.partial(shards, mesh.shape["leaf"]),
        mesh=mesh,
        in_specs=placed,
        out_specs=P("rhs", "leaf", None),
        check_vma=False,
    )
```

```python
import functools

import jax
import jax.numpy as jnp
from jax import lax
from jax.experimental import pallas as pl
from jax.experimental.pallas import tpu as pltpu
from jax.sharding import PartitionSpec as P

BF = jnp.bfloat16
F32 = jnp.float32
MESH = pl.DeviceIdType.MESH
NT = (((1,), (1,)), ((), ()))
NN = (((1,), (0,)), ((), ()))
ORDER = (12, 13, 8, 9, 10, 11, 0, 1, 2, 3, 4, 5, 6, 7)
CHUNKS = (2, 2)


def dot(a, b, dims=NN):
    return lax.dot_general(a, b, dims, preferred_element_type=F32)


def iota(shape, axis):
    return lax.broadcasted_iota(jnp.int32, shape, axis)


def kernel(
    n_leaf,
    near_send_h,
    coup_send_h,
    near_slot_h,
    coup_slot_h,
    density_h,
    near_h,
    col_h,
    up_h,
    coupling_h,
    down_h,
    row_h,
    out,
    near_send,
    coup_send,
    near_slot,
    coup_slot,
    density,
    near,
    col,
    up,
    coupling,
    down,
    row,
    slots,
    slots_s,
    tiles,
    charges,
    table_a,
    table_b,
    send1,
    send2,
    recv2,
    send4,
    recv4,
    in_sem,
    near_sem,
    smem_sem,
    s0_send,
    s0_recv,
    s1_send,
    s1_recv,
    s2_send,
    s2_recv,
    s4_send,
    s4_recv,
):
    me = lax.axis_index("leaf")
    y = lax.axis_index("rhs")
    first = (
        (density_h, density),
        (col_h, col),
        (near_send_h, near_send),
        (coup_send_h, coup_send),
        (near_slot_h, near_slot),
        (coup_slot_h, coup_slot),
        (up_h, up),
    )
    later = ((coupling_h, coupling), (down_h, down), (row_h, row))
    loads = [pltpu.make_async_copy(a, b, in_sem.at[i]) for i, (a, b) in enumerate(first + later)]
    for load in loads[:7]:
        load.start()

    barrier = pltpu.get_barrier_semaphore()
    zs = [lax.rem(me // 8 + dz, n_leaf // 8) * 8 for dz in range(n_leaf // 8)]
    xs = [lax.rem(me // 2 % 4 + w // 2, 4) * 2 + lax.rem(me % 2 + w % 2, 2) for w in range(8)]
    far_z = sorted(range(n_leaf // 8), key=lambda dz: -min(dz, n_leaf // 8 - dz))
    far_x = (5, 4, 3, 2, 7, 6, 1, 0)
    for dz, w in [(dz, w) for dz in far_z for w in far_x if dz or w]:
        pl.semaphore_signal(barrier, inc=1, device_id={"leaf": zs[dz] + xs[w]}, device_id_type=MESH)
    for e in range(1, 4):
        pl.semaphore_signal(barrier, inc=1, device_id={"rhs": lax.rem(y + e, 4)}, device_id_type=MESH)

    blocks = [pltpu.make_async_copy(near_h.at[i], near.at[i], near_sem.at[i]) for i in range(8)]
    for load in loads[7:] + blocks:
        load.start()

    for load in loads[:7]:
        load.wait()
    slots[0, :, :] = jnp.zeros((8, 128), jnp.int32)
    slots[0, 0:4, 0:8] = near_slot[...]
    slots[0, 4:8, 0:14] = coup_slot[...]

    flat = density[...].reshape(32, 384)
    stacked = jnp.concatenate([flat[:, 128 * c : 128 * c + 128] for c in range(3)], axis=0)
    r, q = iota((128, 96), 0), iota((128, 96), 1)
    source = r % 4 * 8 + r % 64 // 8
    pick = (r < 64) & (r % 8 < 4) & (q == source) | (r >= 64) & (q == source + 32 + r // 4 % 2 * 32)
    tile = dot(jnp.where(pick, 1.0, 0.0).astype(BF), stacked)
    r, q = iota((128, 32), 0), iota((128, 32), 1)
    pick = (r % 16 >= 4) & (r % 16 < 8) & (q == r % 4 * 8 + r // 16)
    low = dot(jnp.where(pick, 1.0, 0.0).astype(BF), flat).astype(BF)
    left = iota((16, 128), 1) < 64

    def twice(a):
        return jnp.concatenate([a, a], axis=0)

    level = [dot(low[16 * i : 16 * i + 16], twice(col[i]), NT) for i in range(8)]
    level_values = [a.astype(BF).astype(F32) for a in level]
    for base, count in ((0, 4), (4, 2)):
        level = [
            dot(
                jnp.where(left, level[2 * j].astype(BF).astype(F32), level[2 * j + 1].astype(BF).astype(F32)).astype(BF),
                twice(up[base + j]),
                NT,
            )
            for j in range(count)
        ]
        level_values += [a.astype(BF).astype(F32) for a in level]
    for i in range(14):
        value = level_values[i][:8]
        charges[i] = value.astype(BF)
        if i < 8:
            tiles[0, i] = tile[8 * i : 8 * i + 8].astype(BF)
            tiles[1, i] = tile[64 + 8 * i : 72 + 8 * i].astype(BF)
            table_b[i] = tile[64 + 8 * i : 72 + 8 * i].astype(BF)
            value += tile[8 * i : 8 * i + 8]
        table_a[i] = value.astype(BF)

    def listed(peer, _):
        leaf = near_send[0, 0, peer]
        send1[0, peer] = tiles[0, leaf] + charges[coup_send[0, 0, peer]]
        send1[1, peer] = tiles[1, leaf]
        return 0

    lax.fori_loop(0, n_leaf, listed, 0, unroll=8)
    pl.semaphore_wait(barrier, n_leaf + 2)

    slot_copies = [
        pltpu.make_async_remote_copy(
            slots.at[0],
            slots.at[e],
            s0_send.at[e - 1],
            s0_recv.at[e - 1],
            device_id={"rhs": lax.rem(y + e, 4)},
            device_id_type=MESH,
        )
        for e in range(1, 4)
    ]
    for copy in slot_copies:
        copy.start()

    tables = ((table_a, 14), (table_b, 8))
    for half, (table, own) in enumerate(tables):
        for dz, w in [(dz, w) for w in (far_x, far_x[::-1])[half] for dz in far_z if dz or w]:
            peer = zs[dz] + xs[w]
            pltpu.make_async_remote_copy(
                send1.at[half, peer],
                table.at[own + me],
                s1_send.at[half],
                s1_recv.at[half],
                device_id={"leaf": peer},
                device_id_type=MESH,
            ).start()
        table[own + me] = send1[half, me]

    for copy in slot_copies:
        copy.wait_recv()
    to_smem = pltpu.make_async_copy(slots, slots_s, smem_sem)
    to_smem.start()
    to_smem.wait()

    everything = [
        pltpu.make_async_remote_copy(
            send1.at[half, pl.ds(0, n_leaf - 1)],
            table.at[pl.ds(own, n_leaf - 1)],
            s1_send.at[half],
            s1_recv.at[half],
            device_id={"leaf": lax.rem(me + 1, n_leaf)},
            device_id_type=MESH,
        )
        for half, (table, own) in enumerate(tables)
    ]

    rows, lanes = iota((8, 128), 0), iota((8, 128), 1)
    mask_n = jnp.where(rows < 4, 1.0, 0.0).astype(BF)
    mask_a = jnp.where((rows >= 4) & (lanes < 64), 1.0, 0.0).astype(BF)
    mask_b = jnp.where((rows >= 4) & (lanes >= 64), 1.0, 0.0).astype(BF)

    def read(half, e, i):
        slot = slots_s[e, i % 4, i // 4]
        if half == 1:
            return table_b[slot]
        value = table_a[slot + jnp.where(slot >= 8, 6, 0)] * mask_n
        if i < 28:
            g, k = ORDER[i // 2], i % 2 * 2
            value += table_a[slots_s[e, 4 + k, g]] * mask_a + table_a[slots_s[e, 5 + k, g]] * mask_b
        return value

    sends = [[], []]
    for half in range(2):
        everything[half].wait_recv()
        per = 32 // CHUNKS[half]
        for chunk in range(CHUNKS[half]):
            span = pl.ds(chunk * per, per)
            for e in (1, 3, 2):
                for i in range(chunk * per, chunk * per + per):
                    send2[half, e - 1, i] = read(half, 4 - e, i)
                copy = pltpu.make_async_remote_copy(
                    send2.at[half, e - 1, span],
                    recv2.at[half, e, span],
                    s2_send.at[half, e - 1, chunk],
                    s2_recv.at[half, e - 1, chunk],
                    device_id={"rhs": lax.rem(y + e, 4)},
                    device_id_type=MESH,
                )
                copy.start()
                sends[half].append(copy)
        for i in range(32):
            recv2[half, 0, i] = read(half, 0, i)

    for load in loads[7:]:
        load.wait()

    top = iota((8, 128), 0) < 4

    def regroup(half, i):
        x = [recv2[half, e, i].astype(F32) for e in range(4)]
        z = [pltpu.roll(p, 4, 0) for p in x]
        groups = (
            [jnp.where(top, x[0], z[1]), jnp.where(top, x[2], z[3])],
            [jnp.where(top, z[0], x[1]), jnp.where(top, z[2], x[3])],
        )
        return [jnp.concatenate(g, axis=0).astype(BF) for g in groups]

    def arrived(half, chunk):
        for copy in sends[half][3 * chunk : 3 * chunk + 3]:
            copy.wait_recv()
        return range(chunk * 8 // CHUNKS[half], (chunk + 1) * 8 // CHUNKS[half])

    pairs, total = {}, []
    for chunk in range(CHUNKS[0]):
        for leaf in arrived(0, chunk):
            blocks[leaf].wait()
            value = None
            for k in (0, 2):
                one, two = regroup(0, 4 * leaf + k), regroup(0, 4 * leaf + k + 1)
                pairs[4 * leaf + k], pairs[4 * leaf + k + 1] = one[1], two[1]
                part = dot(
                    jnp.concatenate([one[0], two[0]], axis=1),
                    jnp.concatenate([near[leaf, k, :, 0:128], near[leaf, k + 1, :, 0:128]], axis=1),
                    NT,
                )
                value = part if value is None else value + part
            total.append(value)

    field = {}
    for j, g in enumerate(ORDER):
        field[g] = dot(jnp.concatenate([pairs[2 * j], pairs[2 * j + 1]], axis=1), coupling[g], NT)
    for base, children, count, first in ((12, 8, 2, 4), (8, 0, 4, 0)):
        for j in range(count):
            both = dot(field[base + j].astype(BF), down[first + j])
            field[children + 2 * j] += both[:, :64]
            field[children + 2 * j + 1] += both[:, 64:]
    for i in range(8):
        total[i] += dot(field[i].astype(BF), row[i])

    for chunk in range(CHUNKS[1]):
        for leaf in arrived(1, chunk):
            for k in range(4):
                total[leaf] += dot(
                    jnp.concatenate(regroup(1, 4 * leaf + k), axis=1), near[leaf, k, :, 128:384], NT
                )
    whole = jnp.concatenate([value.astype(BF) for value in total], axis=0)
    r, q = iota((128, 128), 0), iota((128, 128), 1)
    pick = q == r % 8 * 16 + r // 32 * 4 + r // 8 % 4
    sorted_rows = dot(jnp.where(pick, 1.0, 0.0).astype(BF), whole)
    last = []
    for e in (2, 1, 3):
        send4[e - 1] = sorted_rows[32 * e : 32 * e + 32].astype(BF)
        copy = pltpu.make_async_remote_copy(
            send4.at[e - 1],
            recv4.at[3 - e],
            s4_send.at[e - 1],
            s4_recv.at[3 - e],
            device_id={"rhs": lax.rem(y + 4 - e, 4)},
            device_id_type=MESH,
        )
        copy.start()
        last.append(copy)
    for copy in last:
        copy.wait()
    result = sorted_rows[:32]
    for e in range(3):
        result += recv4[e].astype(F32)
    out[...] = result.astype(BF).reshape(4, 8, 384)

    for copy in slot_copies:
        copy.wait_send()
    for copy in everything + sends[0] + sends[1]:
        copy.wait_send()


def shards(n_leaf, density, near_blocks, near_send, near_slot, col, up, coupling, down, row, coup_send, coup_slot):
    vmem = pl.BlockSpec(memory_space=pltpu.VMEM)
    hbm = pl.BlockSpec(memory_space=pl.ANY)
    big = [density, near_blocks, col, up, coupling, down, row]
    dma = pltpu.SemaphoreType.DMA
    return pl.pallas_call(
        functools.partial(kernel, n_leaf),
        out_shape=jax.ShapeDtypeStruct((4, 8, 384), BF),
        in_specs=[hbm] * (4 + len(big)),
        out_specs=vmem,
        scratch_shapes=[
            pltpu.SMEM((1, 1, n_leaf), jnp.int32),
            pltpu.SMEM((1, 1, n_leaf), jnp.int32),
            pltpu.VMEM((4, 8), jnp.int32),
            pltpu.VMEM((4, 14), jnp.int32),
        ]
        + [pltpu.VMEM(a.shape, a.dtype) for a in big]
        + [
            pltpu.VMEM((4, 8, 128), jnp.int32),
            pltpu.SMEM((4, 8, 128), jnp.int32),
            pltpu.VMEM((2, 8, 8, 128), BF),
            pltpu.VMEM((14, 8, 128), BF),
            pltpu.VMEM((14 + n_leaf, 8, 128), BF),
            pltpu.VMEM((8 + n_leaf, 8, 128), BF),
            pltpu.VMEM((2, n_leaf, 8, 128), BF),
            pltpu.VMEM((2, 3, 32, 8, 128), BF),
            pltpu.VMEM((2, 4, 32, 8, 128), BF),
            pltpu.VMEM((3, 32, 384), BF),
            pltpu.VMEM((3, 32, 384), BF),
            dma((10,)),
            dma((8,)),
            dma,
            dma((3,)),
            dma((3,)),
            dma((2,)),
            dma((2,)),
            dma((2, 3, max(CHUNKS))),
            dma((2, 3, max(CHUNKS))),
            dma((3,)),
            dma((3,)),
        ],
        compiler_params=pltpu.CompilerParams(
            collective_id=0, has_side_effects=True, vmem_limit_bytes=62 * 1024 * 1024
        ),
    )(
        jnp.transpose(near_send, (0, 2, 1)),
        jnp.transpose(coup_send, (0, 2, 1)),
        near_slot.T,
        coup_slot.T,
        *big,
    )


def solution(mesh):
    placed = (
        P("rhs", "leaf", None),
        P("leaf", "rhs", None, None),
        P("leaf", None, None),
        P("leaf", "rhs"),
        P("leaf", None, None),
        P("leaf", None, None),
        P("leaf", None, "rhs"),
        P("leaf", None, None),
        P("leaf", None, None),
        P("leaf", None, None),
        P("leaf", "rhs"),
    )
    return jax.shard_map(
        functools.partial(shards, mesh.shape["leaf"]),
        mesh=mesh,
        in_specs=placed,
        out_specs=P("rhs", "leaf", None),
        check_vma=False,
    )
```
